32 devices in a mesh: qry: 8 (over z, core), lib: 4 (over y, x).
Axes of the slice: x: 2, y: 2, z: 4, core: 2. Of those that a mesh axis runs over, the one named last changes fastest.
Arguments:
- query_prints: bfloat16 [256, 2048], P('qry'), may hold values from -500 to 500, as said below
- library_prints: bfloat16 [24576, 2048], P(('lib', 'qry')), may hold values from -1500 to 1500
- query_atoms: float32 [256, 192], P(('qry', 'lib')), may hold values from -3 to 3, as said below
- conformer_atoms: float32 [24576, 192], P(('lib', 'qry')), may hold values from -3 to 3, as said below
- candidates: int32 [256, 64], P(('qry', 'lib')), may hold values from 0 to 24575, as said below
- candidate_count: int32 [256], P(('qry', 'lib')), may hold values from 16 to 64
- home_row: int32 [24576], replicated, may hold values from 0 to 24575, as said below
Outputs:
- tversky: bfloat16 [256, 24576], P(None, ('lib', 'qry'))
- rescore: float32 [256, 64], P(('qry', 'lib'))
The draws below stay inside these ranges and needn't reach their ends.
Inputs may be any that keep to these rules, and one draw needn't show every extreme that they name: query_prints rows and columns carry independent positive scales. `query_atoms`: each row holds x, y and z of 48 atom slots, then their weights; a padded slot has weight 0, and every row has at least one atom of positive weight. `conformer_atoms`: each row holds x, y and z of 48 atom slots, then their weights; a padded slot has weight 0, and every row has at least one atom of positive weight. Among the candidates in the rows of one device (8 queries, padding included), at most 36 have storage rows in any one block of rows b * 768 to (b + 1) * 768 - 1; in every draw some such block receives exactly 36 from the rows of every device. `home_row`: a permutation of 0 to 24575.
All inputs are finite; a program needn't handle non-finite values.
Results may differ from the reference program's by a relative error of at most 0.0029.
Values may be sent and summed in bfloat16 or wider, within the bound.
A program may use at most 64 MiB of HBM per device.

```python
import math
import jax
import jax.numpy as jnp
from jax import lax

F = 2048
ATOMS = 48
CAND = 64
QRY_DEV = 8
LIB_SH = 768
Q = 256
LIB = 24576
CAP = 36


def home_table(key):
    return jax.random.permutation(jax.random.fold_in(key, 11), LIB).astype(jnp.int32)


def draw_home_row(key, part):
    return home_table(key)


def draw_candidates(key, part):
    devices = Q // QRY_DEV
    pairs = QRY_DEV * CAND
    inverse = jnp.argsort(home_table(key), stable=True).astype(jnp.int32)
    base = jax.random.fold_in(key, 23)
    hottest = jax.random.randint(jax.random.fold_in(base, 1), (), 0, devices)
    offsets = jax.random.randint(jax.random.fold_in(base, 2), (devices, 1), 0, devices - 1)
    order = jnp.arange(pairs, dtype=jnp.int32)[None, :]
    others = (offsets + order - CAP) % (devices - 1)
    others = others + (others >= hottest).astype(jnp.int32)
    owner_by_rank = jnp.where(order < CAP, hottest, others)
    keys = jax.random.split(jax.random.fold_in(base, 3), devices)
    shuffles = jax.vmap(lambda single: jax.random.permutation(single, pairs))(keys)
    ranks = jnp.argsort(shuffles, axis=1, stable=True)
    owners = jnp.take_along_axis(owner_by_rank, ranks, axis=1)
    within = jax.random.randint(jax.random.fold_in(base, 4), (devices, pairs), 0, LIB_SH)
    stored = owners * LIB_SH + within
    return inverse[stored].reshape(Q, CAND).astype(jnp.int32)


def draw_query_prints(key, part):
    row_scale = jnp.exp(jax.random.uniform(jax.random.fold_in(key, 1), (Q, 1), minval=0.0, maxval=math.log(10.0)))
    col_scale = jnp.exp(jax.random.uniform(jax.random.fold_in(key, 2), (1, F), minval=0.0, maxval=math.log(10.0)))
    noise = jnp.clip(jax.random.normal(jax.random.fold_in(key, 3), (Q, F)), -5.0, 5.0)
    return (noise * row_scale * col_scale).astype(jnp.bfloat16)


def draw_library_prints(key, part):
    row_scale = jnp.exp(jax.random.uniform(jax.random.fold_in(key, 1), (LIB, 1), minval=math.log(100.0), maxval=math.log(300.0)))
    noise = jnp.clip(jax.random.normal(jax.random.fold_in(key, 3), (LIB, F)), -5.0, 5.0)
    return (noise * row_scale).astype(jnp.bfloat16)


def pack_atoms(key, places, weights, fewest):
    rows = places.shape[0]
    counts = jax.random.randint(jax.random.fold_in(key, 9), (rows, 1, 1), fewest, ATOMS + 1)
    live = (jnp.arange(ATOMS)[None, None, :] < counts).astype(jnp.float32)
    return jnp.concatenate([places, weights * live], axis=1).reshape(rows, 4 * ATOMS)


def draw_query_atoms(key, part):
    places = jax.random.uniform(jax.random.fold_in(key, 1), (Q, 3, ATOMS), minval=-3.0, maxval=3.0)
    weights = jax.random.uniform(jax.random.fold_in(key, 2), (Q, 1, ATOMS), minval=0.5, maxval=1.5)
    return pack_atoms(key, places, weights, max(1, ATOMS // 6))


def draw_conformer_atoms(key, part):
    places = jax.random.uniform(jax.random.fold_in(key, 1), (LIB, 3, ATOMS), minval=-3.0, maxval=3.0)
    weights = jax.random.uniform(jax.random.fold_in(key, 2), (LIB, 1, ATOMS), minval=0.5, maxval=1.5)
    return pack_atoms(key, places, weights, max(1, ATOMS // 2))


def plant(values, own_key, least, high):
    index_at = [jax.random.randint(jax.random.fold_in(own_key, axis), (), 0, length) for axis, length in enumerate(values.shape)]
    main_axis = values.shape.index(max(values.shape))
    neighbour = index_at[:main_axis] + [(index_at[main_axis] + 1) % values.shape[main_axis]] + index_at[main_axis + 1:]
    return values.at[tuple(index_at)].set(least).at[tuple(neighbour)].set(high)


def setup_inputs(seed: int = 0) -> dict:
    splits = jax.random.split(jax.random.key(seed), 8)
    query_prints = draw_query_prints(jax.random.fold_in(splits[7], 71), 0)
    library_prints = draw_library_prints(jax.random.fold_in(splits[7], 71), 0)
    query_atoms = draw_query_atoms(jax.random.fold_in(splits[7], 71), 0)
    conformer_atoms = draw_conformer_atoms(jax.random.fold_in(splits[7], 71), 0)
    candidates = draw_candidates(jax.random.fold_in(splits[7], 71), 0)
    candidate_count = plant(jax.random.randint(splits[5], (Q,), CAND // 4, CAND + 1), jax.random.fold_in(splits[5], 1), CAND // 4, CAND).astype(jnp.int32)
    home_row = draw_home_row(jax.random.fold_in(splits[7], 71), 0)
    return dict(query_prints=query_prints, library_prints=library_prints, query_atoms=query_atoms, conformer_atoms=conformer_atoms, candidates=candidates, candidate_count=candidate_count, home_row=home_row)


SHARPNESS = 0.8
EPSILON = 1e-6


def screen_rows(piece, library):
    scores = lax.dot_general(piece, library, (((1,), (1,)), ((), ())), preferred_element_type=jnp.float32)
    norms = jnp.sum(jnp.square(piece.astype(jnp.float32)), axis=1, keepdims=True)
    return (scores / (norms + EPSILON)).astype(jnp.bfloat16)


def to_atoms(flat):
    return flat.reshape(flat.shape[0], 4, -1).transpose(1, 2, 0)


def intersection(first, second):
    dist = jnp.square(first[0][:, None, :] - second[0][None, :, :])
    dist = dist + jnp.square(first[1][:, None, :] - second[1][None, :, :])
    dist = dist + jnp.square(first[2][:, None, :] - second[2][None, :, :])
    return jnp.sum(first[3][:, None, :] * second[3][None, :, :] * jnp.exp(-SHARPNESS * dist), axis=(0, 1))


def reference(query_prints, library_prints, query_atoms, conformer_atoms, candidates, candidate_count, home_row):
    blocks = query_prints.reshape(8, -1, query_prints.shape[1])
    tversky = lax.map(lambda block: screen_rows(block, library_prints), blocks).reshape(query_prints.shape[0], -1)
    stored = home_row[candidates]
    n_blocks = Q // QRY_DEV

    def rescore_block(args):
        frag_rows, block_rows, counts, block_queries = args
        flat_rows = block_rows.reshape(-1)
        conformer = to_atoms(conformer_atoms[flat_rows])
        fragment = to_atoms(jnp.repeat(frag_rows, CAND, axis=0))
        cross = intersection(fragment, conformer)
        conformer_self = intersection(conformer, conformer)
        frag_atoms = to_atoms(frag_rows)
        query_self = jnp.repeat(intersection(frag_atoms, frag_atoms), CAND)
        prior = tversky[jnp.repeat(block_queries, CAND), flat_rows].astype(jnp.float32)
        shape = cross / (query_self + conformer_self - cross)
        live = jnp.arange(CAND, dtype=jnp.int32)[None, :] < counts[:, None]
        return jnp.where(live, (shape + prior).reshape(-1, CAND), 0.0)

    result = lax.map(rescore_block, (query_atoms.reshape(n_blocks, QRY_DEV, -1), stored.reshape(n_blocks, QRY_DEV, CAND), candidate_count.reshape(n_blocks, QRY_DEV), jnp.arange(Q, dtype=jnp.int32).reshape(n_blocks, QRY_DEV)))
    return tversky, result.reshape(Q, CAND)
```

```python
import functools
import math

import jax
import jax.numpy as jnp
from jax import lax
from jax.experimental import pallas as pl
from jax.experimental.pallas import tpu as pltpu
from jax.sharding import PartitionSpec as P

SHARPNESS = 0.8
EPSILON = 1e-06
LANES = 128
CORES = 2
SCALE = SHARPNESS * math.log2(math.e)
ROOT = math.sqrt(2.0 * SCALE)

F32 = jnp.float32
BF16 = jnp.bfloat16
I32 = jnp.int32


def nt(a, b):
    return lax.dot_general(a, b, (((1,), (1,)), ((), ())), preferred_element_type=F32)


def nn(a, b):
    return lax.dot_general(a, b, (((1,), (0,)), ((), ())), preferred_element_type=F32)


def split2(x):
    hi = x.astype(BF16)
    return hi, (x - hi.astype(F32)).astype(BF16)


def iota(shape, dim):
    return lax.broadcasted_iota(I32, shape, dim)


def fdiv(x, by):
    return jnp.floor((x.astype(F32) + 0.5) * (1.0 / by)).astype(I32)


def prepare(x, y, z, w):
    norm = SCALE * (x * x + y * y + z * z)
    return x * ROOT, y * ROOT, z * ROOT, w * jnp.exp2(-norm)


def self_overlap(ref, lanes, atoms):
    blocks = atoms // 8
    comp = [[ref[pl.ds(c * atoms + 8 * i, 8), lanes] for i in range(blocks)] for c in range(4)]
    total = None
    diag = [None] * blocks
    off = [None] * blocks
    for a in range(atoms):
        xa, ya, za, wa = (ref[pl.ds(c * atoms + a, 1), lanes] for c in range(4))
        wa2 = wa + wa
        for i in range(a // 8, blocks):
            e = jnp.exp2(xa * comp[0][i] + ya * comp[1][i] + za * comp[2][i])
            if i == a // 8:
                diag[i] = wa * e if diag[i] is None else diag[i] + wa * e
            else:
                off[i] = wa2 * e if off[i] is None else off[i] + wa2 * e
    for i in range(blocks):
        part = diag[i] if off[i] is None else diag[i] + off[i]
        part = part * comp[3][i]
        total = part if total is None else total + part
    return jnp.sum(total, axis=0, keepdims=True)


def cross_overlap(qref, cref, lanes, atoms):
    comp = [cref[pl.ds(c * atoms, atoms), lanes] for c in range(4)]
    acc = None
    for a in range(atoms):
        xa, ya, za, wa = (qref[pl.ds(c * atoms + a, 1), lanes] for c in range(4))
        e = wa * jnp.exp2(xa * comp[0] + ya * comp[1] + za * comp[2])
        acc = e if acc is None else acc + e
    return jnp.sum(acc * comp[3], axis=0, keepdims=True)


def kernel(
    nq, nl, cap, id_bytes,
    qp_ref, lib_hbm, qa_ref, conf_hbm, cand_ref, count_ref, home_ref,
    tv_ref, out_ref,
    lib, conf, gath, pack, atoms_in, bucket, codes_in, ret_out, ret_in,
    confp, qprep, pairs_c, pairs_q, onehot, qonehot, cself, qself, shape_s, valid_s,
    loc_sem, s1_send, s1_recv, sib_send, sib_recv, s2_send, s2_recv,
    at_send, at_recv, co_send, co_recv, re_send, re_recv,
):
    q = lax.axis_index("qry")
    l = lax.axis_index("lib")
    dev = nq * nl
    me = q * nl + l
    nz = nq // CORES
    z, c = q // CORES, lax.rem(q, CORES)
    sib = z * CORES + (1 - c)
    own_rows = lib.shape[0]
    block = qp_ref.shape[0]
    cols = gath.shape[2]
    local_q, listed = cand_ref.shape
    cand_n = local_q * listed
    atoms = qa_ref.shape[1] // 4
    half = 2 * atoms
    pairs = onehot.shape[1]

    def target(d):
        t = lax.rem(me + d, dev)
        return t, {"qry": t // nl, "lib": lax.rem(t, nl)}

    barrier = pltpu.get_barrier_semaphore()

    def greet(d, carry):
        _, where = target(d)
        pl.semaphore_signal(barrier, inc=1, device_id=where, device_id_type=pl.DeviceIdType.MESH)
        return carry

    lax.fori_loop(1, dev, greet, 0)

    lib_copy = pltpu.make_async_copy(lib_hbm, lib, loc_sem.at[0])
    conf_copy = pltpu.make_async_copy(conf_hbm, conf, loc_sem.at[1])
    conf_copy.start()
    lib_copy.start()

    qa = qa_ref[...]
    zero = jnp.zeros((local_q, LANES - half), F32)
    top = jnp.concatenate([qa[:, :half], zero], axis=1)
    low = jnp.concatenate([qa[:, half:], zero], axis=1)
    pack[...] = jnp.concatenate([top, low], axis=0).astype(BF16)

    ids = jnp.concatenate([cand_ref[pl.ds(i, 1), :] for i in range(local_q)], axis=1)
    table = home_ref[...]
    trows = table.shape[0]
    pieces = [
        jnp.transpose(((table >> (8 * k)) & 255).astype(F32)).astype(BF16) for k in range(id_bytes)
    ]
    row_hot = jnp.where(iota((trows, cand_n), 0) == (ids >> 7), 1.0, 0.0).astype(BF16)
    lane_hot = iota((LANES, cand_n), 0) == (ids & 127)
    stored = jnp.zeros((1, cand_n), I32)
    for k in range(id_bytes):
        found = nn(pieces[k], row_hot)
        byte = jnp.sum(jnp.where(lane_hot, found, 0.0), axis=0, keepdims=True)
        stored = stored + (byte.astype(I32) << (8 * k))
    owner = fdiv(stored, own_rows)
    slot = stored - owner * own_rows
    owner_l = fdiv(owner, nq)
    owner_s = (owner - owner_l * nq) * nl + owner_l

    owns = iota((dev, cand_n), 0) == owner_s
    owns_b = jnp.where(owns, 1.0, 0.0).astype(BF16)
    tri = jnp.where(iota((cand_n, cand_n), 0) < iota((cand_n, cand_n), 1), 1.0, 0.0).astype(BF16)
    before = nn(owns_b, tri)
    rank = jnp.sum(jnp.where(owns, before, 0.0), axis=0, keepdims=True).astype(I32)
    rank_hot = iota((LANES, cand_n), 0) == rank
    rank_b = jnp.where(rank_hot, 1.0, 0.0).astype(BF16)
    code = slot * local_q + fdiv(iota((1, cand_n), 1), listed) + 1
    lo = (code & 127).astype(F32)
    hi = (code >> 7).astype(F32)
    left = jnp.concatenate([jnp.where(owns, lo, 0.0), jnp.where(owns, hi, 0.0)], axis=0).astype(BF16)
    sums = nt(left, rank_b).astype(I32)
    codes = sums[:dev] + (sums[dev:] << 7)
    for o in range(dev):
        bucket[o] = codes[o : o + 1]

    pl.semaphore_wait(barrier, dev - 1)

    def remote(src, dst, ssem, rsem, dq, dl):
        return pltpu.make_async_remote_copy(
            src_ref=src, dst_ref=dst, send_sem=ssem, recv_sem=rsem,
            device_id={"qry": dq, "lib": dl}, device_id_type=pl.DeviceIdType.MESH,
        )

    def piece(bq, k):
        return gath.at[k, pl.ds(pl.multiple_of(bq * block, block), block), :]

    def stage1(d):
        return remote(
            qp_ref.at[:, pl.ds(pl.multiple_of(l * cols, cols), cols)], piece(q, l),
            s1_send.at[d], s1_recv.at[d], lax.rem(z + d, nz) * CORES + c, l,
        )

    def from_z(d):
        return lax.rem(z - d + nz, nz) * CORES + c

    def stage2(d, e):
        there = piece(from_z(d), l)
        return remote(there, there, s2_send.at[d, e], s2_recv.at[d, e], q, lax.rem(l + e, nl))

    def to_sib(bq, k, i, j):
        there = piece(bq, k)
        return remote(there, there, sib_send.at[i, j], sib_recv.at[i, j], sib, l)

    def from_l(e):
        return lax.rem(l - e + nl, nl)

    def sib_block(d):
        return lax.rem(z - d + nz, nz) * CORES + (1 - c)

    for d in range(1, nz):
        stage1(d).start()
    for k in range(nl):
        gath[k, pl.ds(pl.multiple_of(q * block, block), block), :] = qp_ref[:, k * cols : (k + 1) * cols]
    for k in range(nl):
        to_sib(q, k, 0, k).start()

    def pairwise(src, dst, ssem, rsem):
        def make(d):
            t, where = target(d)
            return pltpu.make_async_remote_copy(
                src_ref=src(t), dst_ref=dst, send_sem=ssem.at[d], recv_sem=rsem.at[d],
                device_id=where, device_id_type=pl.DeviceIdType.MESH,
            )
        return make

    send_code = pairwise(lambda t: bucket.at[t], codes_in.at[me], co_send, co_recv)
    send_atom = pairwise(lambda t: pack, atoms_in.at[me], at_send, at_recv)
    send_back = pairwise(lambda t: ret_out.at[t], ret_in.at[me], re_send, re_recv)

    def launch(d, carry):
        send_code(d).start()
        send_atom(d).start()
        return carry

    lax.fori_loop(1, dev, launch, 0)
    codes_in[me] = bucket[me]
    atoms_in[me] = pack[...]

    conf_copy.wait()
    conf_t = jnp.transpose(conf[...])
    comps = prepare(*(conf_t[i * atoms : (i + 1) * atoms] for i in range(4)))
    for i in range(4):
        confp[i * atoms : (i + 1) * atoms] = comps[i]

    def self_step(g, carry):
        lanes = pl.ds(pl.multiple_of(g * LANES, LANES), LANES)
        cself[0:1, lanes] = self_overlap(confp, lanes, atoms)
        return carry

    lax.fori_loop(0, own_rows // LANES, self_step, 0)

    for d in range(1, nz):
        stage1(d).wait_recv()
        for e in range(1, nl):
            stage2(d, e).start()
        to_sib(from_z(d), l, d, 0).start()

    def landed(d, carry):
        send_code(d).wait_recv()
        send_atom(d).wait_recv()
        return carry

    lax.fori_loop(1, dev, landed, 0)

    got = codes_in[...].reshape(dev, LANES)
    pair_at = iota((1, pairs), 1)
    pair_src = fdiv(pair_at, cap)
    pair_j = pair_at - pair_src * cap
    j_hot = jnp.where(iota((LANES, pairs), 0) == pair_j, 1.0, 0.0).astype(BF16)
    src_hot = iota((dev, pairs), 0) == pair_src
    both = jnp.concatenate([got & 127, got >> 7], axis=0).astype(F32).astype(BF16)
    spread = nn(both, j_hot)
    low7 = jnp.sum(jnp.where(src_hot, spread[:dev], 0.0), axis=0, keepdims=True).astype(I32)
    high = jnp.sum(jnp.where(src_hot, spread[dev:], 0.0), axis=0, keepdims=True).astype(I32)
    pcode = low7 + (high << 7)
    valid_s[...] = jnp.where(pcode > 0, 1.0, 0.0)
    pcode = jnp.maximum(pcode - 1, 0)
    pslot = fdiv(pcode, local_q)
    pquery = pair_src * local_q + (pcode - pslot * local_q)
    onehot[...] = jnp.where(iota((own_rows, pairs), 0) == pslot, 1.0, 0.0).astype(BF16)
    qonehot[...] = jnp.where(iota((dev * local_q, pairs), 0) == pquery, 1.0, 0.0).astype(BF16)

    raw = atoms_in[...].astype(F32)
    q_top = jnp.transpose(raw[:, :local_q].reshape(dev * local_q, LANES))
    q_low = jnp.transpose(raw[:, local_q:].reshape(dev * local_q, LANES))
    comps = prepare(q_top[:atoms], q_top[atoms:half], q_low[:atoms], q_low[atoms:half])
    for i in range(4):
        qprep[i * atoms : (i + 1) * atoms] = comps[i]

    def qself_step(g, carry):
        lanes = pl.ds(pl.multiple_of(g * LANES, LANES), LANES)
        qself[0:1, lanes] = self_overlap(qprep, lanes, atoms)
        return carry

    lax.fori_loop(0, dev * local_q // LANES, qself_step, 0)

    pad = jnp.zeros((7, own_rows), F32)
    hi_c, lo_c = split2(jnp.concatenate([confp[...], cself[...], pad], axis=0))
    pairs_c[...] = nn(hi_c, onehot[...]) + nn(lo_c, onehot[...])
    pad = jnp.zeros((7, dev * local_q), F32)
    hi_q, lo_q = split2(jnp.concatenate([qprep[...], qself[...], pad], axis=0))
    pairs_q[...] = nn(hi_q, qonehot[...]) + nn(lo_q, qonehot[...])

    def cross_step(g, carry):
        lanes = pl.ds(pl.multiple_of(g * LANES, LANES), LANES)
        cross = cross_overlap(pairs_q, pairs_c, lanes, atoms)
        selves = pairs_q[4 * atoms : 4 * atoms + 1, lanes] + pairs_c[4 * atoms : 4 * atoms + 1, lanes]
        shape_s[0:1, lanes] = cross / (selves - cross)
        return carry

    groups = pairs // LANES
    first = groups // 3
    lax.fori_loop(0, first, cross_step, 0)

    for d in range(1, nz):
        for e in range(1, nl):
            stage2(d, e).wait_recv()
            to_sib(from_z(d), from_l(e), d, e).start()

    lax.fori_loop(first, groups, cross_step, 0)

    def sib_wait(bq, k, i, j):
        to_sib(bq, k, i, j).wait_recv()

    for k in range(nl):
        sib_wait(sib, k, 0, k)
    for d in range(1, nz):
        sib_wait(sib_block(d), l, d, 0)
        for e in range(1, nl):
            sib_wait(sib_block(d), from_l(e), d, e)
    lib_copy.wait()

    rows = nq * block
    chunk = min(rows, 256)
    priors = None
    for r in range(0, rows, chunk):
        scores = None
        norms = None
        for k in range(nl):
            part = gath[k, r : r + chunk, :]
            prod = nt(part, lib[:, k * cols : (k + 1) * cols])
            wide = part.astype(F32)
            sq = jnp.sum(wide * wide, axis=1, keepdims=True)
            scores = prod if scores is None else scores + prod
            norms = sq if norms is None else norms + sq
        tv = (scores / (norms + EPSILON)).astype(BF16)
        tv_ref[r : r + chunk, :] = tv
        chosen = nn(tv, onehot[...]) * qonehot[r : r + chunk, :].astype(F32)
        chosen = jnp.sum(chosen, axis=0, keepdims=True)
        priors = chosen if priors is None else priors + chosen

    score = jnp.where(valid_s[...] > 0.0, shape_s[...] + priors, 0.0)
    hi_s, lo_s = split2(jnp.where(src_hot, score, 0.0))
    back = nt(hi_s, j_hot) + nt(lo_s, j_hot)
    for s in range(dev):
        ret_out[s] = back[s : s + 1]

    def launch_back(d, carry):
        send_back(d).start()
        return carry

    lax.fori_loop(1, dev, launch_back, 0)
    ret_in[me] = ret_out[me]

    for d in range(1, nz):
        stage1(d).wait_send()
        to_sib(from_z(d), l, d, 0).wait_send()
        for e in range(1, nl):
            stage2(d, e).wait_send()
            to_sib(from_z(d), from_l(e), d, e).wait_send()
    for k in range(nl):
        to_sib(q, k, 0, k).wait_send()

    def settle(d, carry):
        send_code(d).wait_send()
        send_atom(d).wait_send()
        return carry

    lax.fori_loop(1, dev, settle, 0)

    def landed_back(d, carry):
        send_back(d).wait_recv()
        return carry

    lax.fori_loop(1, dev, landed_back, 0)

    came = jnp.transpose(ret_in[...].reshape(dev, LANES))
    hi_b, lo_b = split2(came)
    mine = nn(hi_b, owns_b) + nn(lo_b, owns_b)
    final = jnp.sum(jnp.where(rank_hot, mine, 0.0), axis=0, keepdims=True)
    for i in range(local_q):
        line = final[:, i * listed : (i + 1) * listed]
        live = iota((1, listed), 1) < count_ref[i]
        out_ref[i : i + 1, :] = jnp.where(live, line, 0.0)

    def settle_back(d, carry):
        send_back(d).wait_send()
        return carry

    lax.fori_loop(1, dev, settle_back, 0)


def body(nq, nl, query_prints, library_prints, query_atoms, conformer_atoms, candidates, candidate_count, home_row):
    dev = nq * nl
    block, width = query_prints.shape
    own_rows = library_prints.shape[0]
    local_q, listed = candidates.shape
    atoms = query_atoms.shape[1] // 4
    cand_n = local_q * listed
    cap = 2 * ((cand_n + dev - 1) // dev) + 4
    pairs = (dev * cap + LANES - 1) // LANES * LANES
    id_bytes = ((home_row.shape[0] - 1).bit_length() + 7) // 8
    rows = nq * block
    nz = nq // CORES
    vm = pltpu.VMEM
    dma = pltpu.SemaphoreType.DMA
    vspec = pl.BlockSpec(memory_space=pltpu.VMEM)
    aspec = pl.BlockSpec(memory_space=pl.ANY)
    return pl.pallas_call(
        functools.partial(kernel, nq, nl, cap, id_bytes),
        out_shape=(
            jax.ShapeDtypeStruct((rows, own_rows), BF16),
            jax.ShapeDtypeStruct((local_q, listed), F32),
        ),
        in_specs=[
            vspec, aspec, vspec, aspec, vspec, pl.BlockSpec(memory_space=pltpu.SMEM), vspec,
        ],
        out_specs=(vspec, vspec),
        scratch_shapes=[
            vm((own_rows, width), BF16),
            vm((own_rows, 4 * atoms), F32),
            vm((nl, rows, width // nl), BF16),
            vm((2 * local_q, LANES), BF16),
            vm((dev, 2 * local_q, LANES), BF16),
            vm((dev, 1, LANES), I32),
            vm((dev, 1, LANES), I32),
            vm((dev, 1, LANES), F32),
            vm((dev, 1, LANES), F32),
            vm((4 * atoms, own_rows), F32),
            vm((4 * atoms, rows), F32),
            vm((4 * atoms + 8, pairs), F32),
            vm((4 * atoms + 8, pairs), F32),
            vm((own_rows, pairs), BF16),
            vm((rows, pairs), BF16),
            vm((1, own_rows), F32),
            vm((1, rows), F32),
            vm((1, pairs), F32),
            vm((1, pairs), F32),
            dma((2,)),
            dma((nz,)), dma((nz,)),
            dma((nz, nl)), dma((nz, nl)),
            dma((nz, nl)), dma((nz, nl)),
            dma((dev,)), dma((dev,)),
            dma((dev,)), dma((dev,)),
            dma((dev,)), dma((dev,)),
        ],
        compiler_params=pltpu.CompilerParams(
            collective_id=0, has_side_effects=True, vmem_limit_bytes=56 * 1024 * 1024
        ),
    )(
        query_prints, library_prints, query_atoms, conformer_atoms, candidates, candidate_count,
        home_row.reshape(-1, LANES),
    )


def solution(mesh):
    return jax.shard_map(
        functools.partial(body, mesh.shape["qry"], mesh.shape["lib"]),
        mesh=mesh,
        in_specs=(
            P("qry", None),
            P(("lib", "qry"), None),
            P(("qry", "lib"), None),
            P(("lib", "qry"), None),
            P(("qry", "lib"), None),
            P(("qry", "lib")),
            P(),
        ),
        out_specs=(P(None, ("lib", "qry")), P(("qry", "lib"), None)),
        check_vma=False,
    )
```

```python
import functools
import math

import jax
import jax.numpy as jnp
from jax import lax
from jax.experimental import pallas as pl
from jax.experimental.pallas import tpu as pltpu
from jax.sharding import PartitionSpec as P

SHARPNESS = 0.8
EPSILON = 1e-06
LANES = 128
CORES = 2
SCALE = SHARPNESS * math.log2(math.e)
ROOT = math.sqrt(2.0 * SCALE)

F32 = jnp.float32
BF16 = jnp.bfloat16
I32 = jnp.int32


def nt(a, b):
    return lax.dot_general(a, b, (((1,), (1,)), ((), ())), preferred_element_type=F32)


def nn(a, b):
    return lax.dot_general(a, b, (((1,), (0,)), ((), ())), preferred_element_type=F32)


def split2(x):
    hi = x.astype(BF16)
    return hi, (x - hi.astype(F32)).astype(BF16)


def iota(shape, dim):
    return lax.broadcasted_iota(I32, shape, dim)


def fdiv(x, by):
    return jnp.floor((x.astype(F32) + 0.5) * (1.0 / by)).astype(I32)


def prepare(x, y, z, w):
    norm = SCALE * (x * x + y * y + z * z)
    return x * ROOT, y * ROOT, z * ROOT, w * jnp.exp2(-norm)


def self_overlap(ref, lanes, atoms):
    blocks = atoms // 8
    comp = [[ref[pl.ds(c * atoms + 8 * i, 8), lanes] for i in range(blocks)] for c in range(4)]
    total = None
    diag = [None] * blocks
    off = [None] * blocks
    for a in range(atoms):
        xa, ya, za, wa = (ref[pl.ds(c * atoms + a, 1), lanes] for c in range(4))
        wa2 = wa + wa
        for i in range(a // 8, blocks):
            e = jnp.exp2(xa * comp[0][i] + ya * comp[1][i] + za * comp[2][i])
            if i == a // 8:
                diag[i] = wa * e if diag[i] is None else diag[i] + wa * e
            else:
                off[i] = wa2 * e if off[i] is None else off[i] + wa2 * e
    for i in range(blocks):
        part = diag[i] if off[i] is None else diag[i] + off[i]
        part = part * comp[3][i]
        total = part if total is None else total + part
    return jnp.sum(total, axis=0, keepdims=True)


def cross_overlap(qref, cref, lanes, atoms):
    comp = [cref[pl.ds(c * atoms, atoms), lanes] for c in range(4)]
    acc = None
    for a in range(atoms):
        xa, ya, za, wa = (qref[pl.ds(c * atoms + a, 1), lanes] for c in range(4))
        e = wa * jnp.exp2(xa * comp[0] + ya * comp[1] + za * comp[2])
        acc = e if acc is None else acc + e
    return jnp.sum(acc * comp[3], axis=0, keepdims=True)


def kernel(
    nq, nl, cap, id_bytes,
    qp_ref, lib_hbm, qa_ref, conf_hbm, cand_ref, count_ref, home_ref,
    tv_ref, out_ref,
    lib, conf, gath, pack, atoms_in, bucket, codes_in, ret_out, ret_in,
    confp, qprep, pairs_c, pairs_q, onehot, qonehot, cself, qself, shape_s, valid_s,
    loc_sem, s1_send, s1_recv, sib_send, sib_recv, s2_send, s2_recv,
    at_send, at_recv, co_send, co_recv, re_send, re_recv,
):
    q = lax.axis_index("qry")
    l = lax.axis_index("lib")
    dev = nq * nl
    me = q * nl + l
    nz = nq // CORES
    z, c = q // CORES, lax.rem(q, CORES)
    sib = z * CORES + (1 - c)
    own_rows = lib.shape[0]
    block = qp_ref.shape[0]
    cols = gath.shape[2]
    local_q, listed = cand_ref.shape
    cand_n = local_q * listed
    atoms = qa_ref.shape[1] // 4
    half = 2 * atoms
    pairs = onehot.shape[1]

    def wrap(x, n):
        return jnp.where(x >= n, x - n, x)

    near = [wrap(l + e, nl) for e in range(nl)]

    def others(act):
        for e in range(1, nl):
            act(q * nl + near[e], q, near[e])

        def step(d, carry):
            tq = wrap(q + d, nq)
            for e in range(nl):
                act(tq * nl + near[e], tq, near[e])
            return carry

        lax.fori_loop(1, nq, step, 0)

    def take(ref, sem):
        pltpu.make_async_copy(ref, ref, sem).wait()

    barrier = pltpu.get_barrier_semaphore()

    def greet(t, tq, tl):
        pl.semaphore_signal(
            barrier, inc=1, device_id={"qry": tq, "lib": tl}, device_id_type=pl.DeviceIdType.MESH
        )

    others(greet)

    lib_copy = pltpu.make_async_copy(lib_hbm, lib, loc_sem.at[0])
    conf_copy = pltpu.make_async_copy(conf_hbm, conf, loc_sem.at[1])
    conf_copy.start()
    lib_copy.start()

    qa = qa_ref[...]
    zero = jnp.zeros((local_q, LANES - half), F32)
    top = jnp.concatenate([qa[:, :half], zero], axis=1)
    low = jnp.concatenate([qa[:, half:], zero], axis=1)
    pack[...] = jnp.concatenate([top, low], axis=0).astype(BF16)

    ids = jnp.concatenate([cand_ref[pl.ds(i, 1), :] for i in range(local_q)], axis=1)
    table = home_ref[...]
    trows = table.shape[0]
    pieces = [
        jnp.transpose(((table >> (8 * k)) & 255).astype(F32)).astype(BF16) for k in range(id_bytes)
    ]
    row_hot = jnp.where(iota((trows, cand_n), 0) == (ids >> 7), 1.0, 0.0).astype(BF16)
    lane_hot = iota((LANES, cand_n), 0) == (ids & 127)
    stored = jnp.zeros((1, cand_n), I32)
    for k in range(id_bytes):
        found = nn(pieces[k], row_hot)
        byte = jnp.sum(jnp.where(lane_hot, found, 0.0), axis=0, keepdims=True)
        stored = stored + (byte.astype(I32) << (8 * k))
    owner = fdiv(stored, own_rows)
    slot = stored - owner * own_rows
    owner_l = fdiv(owner, nq)
    owner_s = (owner - owner_l * nq) * nl + owner_l

    pl.semaphore_wait(barrier, dev - 1)

    def remote(src, dst, ssem, rsem, dq, dl):
        return pltpu.make_async_remote_copy(
            src_ref=src, dst_ref=dst, send_sem=ssem, recv_sem=rsem,
            device_id={"qry": dq, "lib": dl}, device_id_type=pl.DeviceIdType.MESH,
        )

    def piece(bq, k):
        return gath.at[k, pl.ds(pl.multiple_of(bq * block, block), block), :]

    def stage1(d):
        return remote(
            qp_ref.at[:, pl.ds(pl.multiple_of(l * cols, cols), cols)], piece(q, l),
            s1_send, s1_recv.at[d], lax.rem(z + d, nz) * CORES + c, l,
        )

    def from_z(d):
        return lax.rem(z - d + nz, nz) * CORES + c

    def stage2(d, e):
        there = piece(from_z(d), l)
        return remote(there, there, s2_send, s2_recv.at[d, e], q, lax.rem(l + e, nl))

    def to_sib(bq, k):
        there = piece(bq, k)
        return remote(there, there, sib_send, sib_recv, sib, l)

    def from_l(e):
        return lax.rem(l - e + nl, nl)

    for d in range(1, nz):
        stage1(d).start()
    for k in range(nl):
        gath[k, pl.ds(pl.multiple_of(q * block, block), block), :] = qp_ref[:, k * cols : (k + 1) * cols]
    for k in range(nl):
        to_sib(q, k).start()

    def pairwise(src, dst, ssem, rsem):
        def start(t, tq, tl):
            remote(src(t), dst, ssem, rsem, tq, tl).start()

        return start

    others(pairwise(lambda t: pack, atoms_in.at[me], at_send, at_recv))
    atoms_in[me] = pack[...]

    owns = iota((dev, cand_n), 0) == owner_s
    owns_b = jnp.where(owns, 1.0, 0.0).astype(BF16)
    tri = jnp.where(iota((cand_n, cand_n), 0) < iota((cand_n, cand_n), 1), 1.0, 0.0).astype(BF16)
    before = nn(owns_b, tri)
    rank = jnp.sum(jnp.where(owns, before, 0.0), axis=0, keepdims=True).astype(I32)
    rank_hot = iota((LANES, cand_n), 0) == rank
    rank_b = jnp.where(rank_hot, 1.0, 0.0).astype(BF16)
    code = slot * local_q + fdiv(iota((1, cand_n), 1), listed) + 1
    lo = (code & 127).astype(F32)
    hi = (code >> 7).astype(F32)
    left = jnp.concatenate([jnp.where(owns, lo, 0.0), jnp.where(owns, hi, 0.0)], axis=0).astype(BF16)
    sums = nt(left, rank_b).astype(I32)
    codes = sums[:dev] + (sums[dev:] << 7)
    for o in range(dev):
        bucket[o] = codes[o : o + 1]

    others(pairwise(lambda t: bucket.at[t], codes_in.at[me], co_send, co_recv))
    codes_in[me] = bucket[me]

    conf_copy.wait()
    comps = prepare(*(conf[i * atoms : (i + 1) * atoms] for i in range(4)))
    for i in range(4):
        confp[i * atoms : (i + 1) * atoms] = comps[i]

    def self_step(g, carry):
        lanes = pl.ds(pl.multiple_of(g * LANES, LANES), LANES)
        cself[0:1, lanes] = self_overlap(confp, lanes, atoms)
        return carry

    lax.fori_loop(0, own_rows // LANES, self_step, 0)

    for d in range(1, nz):
        stage1(d).wait_recv()
        for e in range(1, nl):
            stage2(d, e).start()
        to_sib(from_z(d), l).start()

    rest = pl.ds(0, dev - 1)
    take(codes_in.at[rest], co_recv)
    take(atoms_in.at[rest], at_recv)

    got = codes_in[...].reshape(dev, LANES)
    pair_at = iota((1, pairs), 1)
    pair_src = fdiv(pair_at, cap)
    pair_j = pair_at - pair_src * cap
    j_hot = jnp.where(iota((LANES, pairs), 0) == pair_j, 1.0, 0.0).astype(BF16)
    src_hot = iota((dev, pairs), 0) == pair_src
    both = jnp.concatenate([got & 127, got >> 7], axis=0).astype(F32).astype(BF16)
    spread = nn(both, j_hot)
    low7 = jnp.sum(jnp.where(src_hot, spread[:dev], 0.0), axis=0, keepdims=True).astype(I32)
    high = jnp.sum(jnp.where(src_hot, spread[dev:], 0.0), axis=0, keepdims=True).astype(I32)
    pcode = low7 + (high << 7)
    valid_s[...] = jnp.where(pcode > 0, 1.0, 0.0)
    pcode = jnp.maximum(pcode - 1, 0)
    pslot = fdiv(pcode, local_q)
    pquery = pair_src * local_q + (pcode - pslot * local_q)
    onehot[...] = jnp.where(iota((own_rows, pairs), 0) == pslot, 1.0, 0.0).astype(BF16)
    qonehot[...] = jnp.where(iota((dev * local_q, pairs), 0) == pquery, 1.0, 0.0).astype(BF16)

    raw = atoms_in[...].astype(F32)
    q_top = jnp.transpose(raw[:, :local_q].reshape(dev * local_q, LANES))
    q_low = jnp.transpose(raw[:, local_q:].reshape(dev * local_q, LANES))
    comps = prepare(q_top[:atoms], q_top[atoms:half], q_low[:atoms], q_low[atoms:half])
    for i in range(4):
        qprep[i * atoms : (i + 1) * atoms] = comps[i]

    def qself_step(g, carry):
        lanes = pl.ds(pl.multiple_of(g * LANES, LANES), LANES)
        qself[0:1, lanes] = self_overlap(qprep, lanes, atoms)
        return carry

    lax.fori_loop(0, dev * local_q // LANES, qself_step, 0)

    pad = jnp.zeros((7, own_rows), F32)
    hi_c, lo_c = split2(jnp.concatenate([confp[...], cself[...], pad], axis=0))
    pairs_c[...] = nn(hi_c, onehot[...]) + nn(lo_c, onehot[...])
    pad = jnp.zeros((7, dev * local_q), F32)
    hi_q, lo_q = split2(jnp.concatenate([qprep[...], qself[...], pad], axis=0))
    pairs_q[...] = nn(hi_q, qonehot[...]) + nn(lo_q, qonehot[...])

    def cross_step(g, carry):
        lanes = pl.ds(pl.multiple_of(g * LANES, LANES), LANES)
        cross = cross_overlap(pairs_q, pairs_c, lanes, atoms)
        selves = pairs_q[4 * atoms : 4 * atoms + 1, lanes] + pairs_c[4 * atoms : 4 * atoms + 1, lanes]
        shape_s[0:1, lanes] = cross / (selves - cross)
        return carry

    groups = pairs // LANES
    first = groups // 3
    lax.fori_loop(0, first, cross_step, 0)

    for d in range(1, nz):
        for e in range(1, nl):
            stage2(d, e).wait_recv()
            to_sib(from_z(d), from_l(e)).start()

    lax.fori_loop(first, groups, cross_step, 0)

    take(gath.at[:, pl.ds(0, nz * block), :], sib_recv)
    lib_copy.wait()

    rows = nq * block
    chunk = min(rows, 256)
    priors = None
    for r in range(0, rows, chunk):
        scores = None
        norms = None
        for k in range(nl):
            part = gath[k, r : r + chunk, :]
            prod = nt(part, lib[:, k * cols : (k + 1) * cols])
            wide = part.astype(F32)
            sq = jnp.sum(wide * wide, axis=1, keepdims=True)
            scores = prod if scores is None else scores + prod
            norms = sq if norms is None else norms + sq
        tv = (scores / (norms + EPSILON)).astype(BF16)
        tv_ref[r : r + chunk, :] = tv
        chosen = nn(tv, onehot[...]) * qonehot[r : r + chunk, :].astype(F32)
        chosen = jnp.sum(chosen, axis=0, keepdims=True)
        priors = chosen if priors is None else priors + chosen

    score = jnp.where(valid_s[...] > 0.0, shape_s[...] + priors, 0.0)
    hi_s, lo_s = split2(jnp.where(src_hot, score, 0.0))
    back = nt(hi_s, j_hot) + nt(lo_s, j_hot)
    for s in range(dev):
        ret_out[s] = back[s : s + 1]

    others(pairwise(lambda t: ret_out.at[t], ret_in.at[me], re_send, re_recv))
    ret_in[me] = ret_out[me]

    take(gath.at[0, pl.ds(0, (nz - 1) * block), :], s1_send)
    take(gath.at[pl.ds(0, nl - 1), pl.ds(0, (nz - 1) * block), :], s2_send)
    take(gath.at[:, pl.ds(0, nz * block), :], sib_send)
    take(bucket.at[rest], co_send)
    take(atoms_in.at[rest], at_send)
    take(ret_in.at[rest], re_recv)

    came = jnp.transpose(ret_in[...].reshape(dev, LANES))
    hi_b, lo_b = split2(came)
    mine = nn(hi_b, owns_b) + nn(lo_b, owns_b)
    final = jnp.sum(jnp.where(rank_hot, mine, 0.0), axis=0, keepdims=True)
    for i in range(local_q):
        line = final[:, i * listed : (i + 1) * listed]
        live = iota((1, listed), 1) < count_ref[i]
        out_ref[i : i + 1, :] = jnp.where(live, line, 0.0)

    take(ret_out.at[rest], re_send)


def body(nq, nl, query_prints, library_prints, query_atoms, conformer_atoms, candidates, candidate_count, home_row):
    dev = nq * nl
    block, width = query_prints.shape
    own_rows = library_prints.shape[0]
    local_q, listed = candidates.shape
    atoms = query_atoms.shape[1] // 4
    cand_n = local_q * listed
    cap = 2 * ((cand_n + dev - 1) // dev) + 4
    pairs = (dev * cap + LANES - 1) // LANES * LANES
    id_bytes = ((home_row.shape[0] - 1).bit_length() + 7) // 8
    rows = nq * block
    nz = nq // CORES
    limit = (50 if dev <= 64 else 56) * 1024 * 1024
    vm = pltpu.VMEM
    dma = pltpu.SemaphoreType.DMA
    vspec = pl.BlockSpec(memory_space=pltpu.VMEM)
    aspec = pl.BlockSpec(memory_space=pl.ANY)
    return pl.pallas_call(
        functools.partial(kernel, nq, nl, cap, id_bytes),
        out_shape=(
            jax.ShapeDtypeStruct((rows, own_rows), BF16),
            jax.ShapeDtypeStruct((local_q, listed), F32),
        ),
        in_specs=[
            vspec, aspec, vspec, aspec, vspec, pl.BlockSpec(memory_space=pltpu.SMEM), vspec,
        ],
        out_specs=(vspec, vspec),
        scratch_shapes=[
            vm((own_rows, width), BF16),
            vm((4 * atoms, own_rows), F32),
            vm((nl, rows, width // nl), BF16),
            vm((2 * local_q, LANES), BF16),
            vm((dev, 2 * local_q, LANES), BF16),
            vm((dev, 1, LANES), I32),
            vm((dev, 1, LANES), I32),
            vm((dev, 1, LANES), F32),
            vm((dev, 1, LANES), F32),
            vm((4 * atoms, own_rows), F32),
            vm((4 * atoms, rows), F32),
            vm((4 * atoms + 8, pairs), F32),
            vm((4 * atoms + 8, pairs), F32),
            vm((own_rows, pairs), BF16),
            vm((rows, pairs), BF16),
            vm((1, own_rows), F32),
            vm((1, rows), F32),
            vm((1, pairs), F32),
            vm((1, pairs), F32),
            dma((2,)),
            dma, dma((nz,)),
            dma, dma,
            dma, dma((nz, nl)),
            dma, dma,
            dma, dma,
            dma, dma,
        ],
        compiler_params=pltpu.CompilerParams(
            collective_id=0, has_side_effects=True, vmem_limit_bytes=limit
        ),
    )(
        query_prints, library_prints, query_atoms, conformer_atoms.T, candidates, candidate_count,
        home_row.reshape(-1, LANES),
    )


def solution(mesh):
    return jax.shard_map(
        functools.partial(body, mesh.shape["qry"], mesh.shape["lib"]),
        mesh=mesh,
        in_specs=(
            P("qry", None),
            P(("lib", "qry"), None),
            P(("qry", "lib"), None),
            P(("lib", "qry"), None),
            P(("qry", "lib"), None),
            P(("qry", "lib")),
            P(),
        ),
        out_specs=(P(None, ("lib", "qry")), P(("qry", "lib"), None)),
        check_vma=False,
    )
```

```python
import functools
import math

import jax
import jax.numpy as jnp
from jax import lax
from jax.experimental import pallas as pl
from jax.experimental.pallas import tpu as pltpu
from jax.sharding import PartitionSpec as P

SHARPNESS = 0.8
EPSILON = 1e-06
LANES = 128
CORES = 2
SCALE = SHARPNESS * math.log2(math.e)
ROOT = math.sqrt(2.0 * SCALE)

F32 = jnp.float32
BF16 = jnp.bfloat16
I32 = jnp.int32


def nt(a, b):
    return lax.dot_general(a, b, (((1,), (1,)), ((), ())), preferred_element_type=F32)


def nn(a, b):
    return lax.dot_general(a, b, (((1,), (0,)), ((), ())), preferred_element_type=F32)


def split2(x):
    hi = x.astype(BF16)
    return hi, (x - hi.astype(F32)).astype(BF16)


def iota(shape, dim):
    return lax.broadcasted_iota(I32, shape, dim)


def fdiv(x, by):
    return jnp.floor((x.astype(F32) + 0.5) * (1.0 / by)).astype(I32)


def prepare(x, y, z, w):
    norm = SCALE * (x * x + y * y + z * z)
    return x * ROOT, y * ROOT, z * ROOT, w * jnp.exp2(-norm)


def self_overlap(ref, lanes, atoms):
    blocks = atoms // 8
    comp = [[ref[pl.ds(c * atoms + 8 * i, 8), lanes] for i in range(blocks)] for c in range(4)]
    total = None
    diag = [None] * blocks
    off = [None] * blocks
    for a in range(atoms):
        xa, ya, za, wa = (ref[pl.ds(c * atoms + a, 1), lanes] for c in range(4))
        wa2 = wa + wa
        for i in range(a // 8, blocks):
            e = jnp.exp2(xa * comp[0][i] + ya * comp[1][i] + za * comp[2][i])
            if i == a // 8:
                diag[i] = wa * e if diag[i] is None else diag[i] + wa * e
            else:
                off[i] = wa2 * e if off[i] is None else off[i] + wa2 * e
    for i in range(blocks):
        part = diag[i] if off[i] is None else diag[i] + off[i]
        part = part * comp[3][i]
        total = part if total is None else total + part
    return jnp.sum(total, axis=0, keepdims=True)


def cross_overlap(qref, cref, lanes, atoms):
    comp = [cref[pl.ds(c * atoms, atoms), lanes] for c in range(4)]
    acc = None
    for a in range(atoms):
        xa, ya, za, wa = (qref[pl.ds(c * atoms + a, 1), lanes] for c in range(4))
        e = wa * jnp.exp2(xa * comp[0] + ya * comp[1] + za * comp[2])
        acc = e if acc is None else acc + e
    return jnp.sum(acc * comp[3], axis=0, keepdims=True)


def kernel(
    nq, nl, cap, id_bytes,
    qp_hbm, lib_hbm, qa_hbm, conf_hbm, cand_hbm, count_hbm, home_hbm,
    tv_ref, out_ref,
    qp_ref, qa_ref, cand_ref, count_ref, home_ref,
    lib, conf, gath, pack, atoms_in, bucket, mid, codes_in, ret_out, mid_back, ret_in,
    confp, qprep, pairs_c, pairs_q, onehot, qonehot, cself, qself, shape_s, valid_s,
    loc_sem, s1_send, s1_recv, sib_send, sib_recv, s2_send, s2_recv,
    send_a, recv_a, send_b, recv_b,
):
    q = lax.axis_index("qry")
    l = lax.axis_index("lib")
    dev = nq * nl
    me = q * nl + l
    nz = nq // CORES
    z, c = q // CORES, lax.rem(q, CORES)
    sib = z * CORES + (1 - c)
    own_rows = lib.shape[0]
    block = qp_ref.shape[0]
    cols = gath.shape[2]
    local_q, listed = cand_ref.shape
    cand_n = local_q * listed
    atoms = qa_ref.shape[1] // 4
    half = 2 * atoms
    pairs = onehot.shape[1]

    def wrap(x, n):
        return jnp.where(x >= n, x - n, x)

    lib_peers = [wrap(l + e, nl) for e in range(1, nl)]
    qry_peers = [wrap(q + d, nq) for d in range(1, nq)]

    def take(ref, sem):
        pltpu.make_async_copy(ref, ref, sem).wait()

    barrier = pltpu.get_barrier_semaphore()

    for tq, tl in [(q, t) for t in lib_peers] + [(t, l) for t in qry_peers]:
        pl.semaphore_signal(
            barrier, inc=1, device_id={"qry": tq, "lib": tl}, device_id_type=pl.DeviceIdType.MESH
        )

    loads = [
        pltpu.make_async_copy(src, dst, loc_sem.at[2 + n])
        for n, (src, dst) in enumerate(
            ((qa_hbm, qa_ref), (cand_hbm, cand_ref), (home_hbm, home_ref), (qp_hbm, qp_ref), (count_hbm, count_ref))
        )
    ]
    for load in loads:
        load.start()
    lib_copy = pltpu.make_async_copy(lib_hbm, lib, loc_sem.at[0])
    conf_copy = pltpu.make_async_copy(conf_hbm, conf, loc_sem.at[1])
    conf_copy.start()
    lib_copy.start()

    for load in loads:
        load.wait()

    qa = qa_ref[...]
    zero = jnp.zeros((local_q, LANES - half), F32)
    top = jnp.concatenate([qa[:, :half], zero], axis=1)
    low = jnp.concatenate([qa[:, half:], zero], axis=1)
    pack[...] = jnp.concatenate([top, low], axis=0).astype(BF16)

    ids = jnp.concatenate([cand_ref[pl.ds(i, 1), :] for i in range(local_q)], axis=1)
    table = home_ref[...]
    trows = table.shape[0]
    pieces = [
        jnp.transpose(((table >> (8 * k)) & 255).astype(F32)).astype(BF16) for k in range(id_bytes)
    ]
    row_hot = jnp.where(iota((trows, cand_n), 0) == (ids >> 7), 1.0, 0.0).astype(BF16)
    lane_hot = iota((LANES, cand_n), 0) == (ids & 127)
    stored = jnp.zeros((1, cand_n), I32)
    for k in range(id_bytes):
        found = nn(pieces[k], row_hot)
        byte = jnp.sum(jnp.where(lane_hot, found, 0.0), axis=0, keepdims=True)
        stored = stored + (byte.astype(I32) << (8 * k))
    owner = fdiv(stored, own_rows)
    slot = stored - owner * own_rows

    pl.semaphore_wait(barrier, nq + nl - 2)

    def remote(src, dst, ssem, rsem, dq, dl):
        return pltpu.make_async_remote_copy(
            src_ref=src, dst_ref=dst, send_sem=ssem, recv_sem=rsem,
            device_id={"qry": dq, "lib": dl}, device_id_type=pl.DeviceIdType.MESH,
        )

    def piece(bq, k):
        return gath.at[k, pl.ds(pl.multiple_of(bq * block, block), block), :]

    def stage1(d):
        return remote(
            qp_ref.at[:, pl.ds(pl.multiple_of(l * cols, cols), cols)], piece(q, l),
            s1_send, s1_recv.at[d], lax.rem(z + d, nz) * CORES + c, l,
        )

    def from_z(d):
        return lax.rem(z - d + nz, nz) * CORES + c

    def stage2(d, e):
        there = piece(from_z(d), l)
        return remote(there, there, s2_send, s2_recv.at[d, e], q, lax.rem(l + e, nl))

    def to_sib(bq, k):
        there = piece(bq, k)
        return remote(there, there, sib_send, sib_recv, sib, l)

    def from_l(e):
        return lax.rem(l - e + nl, nl)

    for d in range(1, nz):
        stage1(d).start()
    for k in range(nl):
        gath[k, pl.ds(pl.multiple_of(q * block, block), block), :] = qp_ref[:, k * cols : (k + 1) * cols]
    for k in range(nl):
        to_sib(q, k).start()

    for t in qry_peers:
        remote(pack, atoms_in.at[q, l], send_a.at[0], recv_a.at[0], t, l).start()
    atoms_in[q, l] = pack[...]

    owns = iota((dev, cand_n), 0) == owner
    owns_b = jnp.where(owns, 1.0, 0.0).astype(BF16)
    tri = jnp.where(iota((cand_n, cand_n), 0) < iota((cand_n, cand_n), 1), 1.0, 0.0).astype(BF16)
    before = nn(owns_b, tri)
    rank = jnp.sum(jnp.where(owns, before, 0.0), axis=0, keepdims=True).astype(I32)
    rank_hot = iota((LANES, cand_n), 0) == rank
    rank_b = jnp.where(rank_hot, 1.0, 0.0).astype(BF16)
    code = slot * local_q + fdiv(iota((1, cand_n), 1), listed) + 1
    lo = (code & 127).astype(F32)
    hi = (code >> 7).astype(F32)
    left = jnp.concatenate([jnp.where(owns, lo, 0.0), jnp.where(owns, hi, 0.0)], axis=0).astype(BF16)
    sums = nt(left, rank_b).astype(I32)
    codes = sums[:dev] + (sums[dev:] << 7)
    for o in range(dev):
        bucket[o // nq, o % nq] = codes[o : o + 1]

    for t in lib_peers:
        remote(bucket.at[t], mid.at[l], send_a.at[1], recv_a.at[1], q, t).start()
    mid[l] = bucket[l]

    conf_copy.wait()
    comps = prepare(*(conf[i * atoms : (i + 1) * atoms] for i in range(4)))
    for i in range(4):
        confp[i * atoms : (i + 1) * atoms] = comps[i]

    q_rest = pl.ds(0, nq - 1)
    l_rest = pl.ds(0, nl - 1)
    take(atoms_in.at[q_rest, 0], recv_a.at[0])
    for t in lib_peers:
        remote(atoms_in.at[:, l], atoms_in.at[:, l], send_b.at[0], recv_b.at[0], q, t).start()
    take(mid.at[l_rest], recv_a.at[1])
    for t in qry_peers:
        remote(mid.at[:, t], codes_in.at[q], send_b.at[1], recv_b.at[1], t, l).start()
    for k in range(nl):
        codes_in[q, k] = mid[k, q]

    def self_step(g, carry):
        lanes = pl.ds(pl.multiple_of(g * LANES, LANES), LANES)
        cself[0:1, lanes] = self_overlap(confp, lanes, atoms)
        return carry

    lax.fori_loop(0, own_rows // LANES, self_step, 0)

    for d in range(1, nz):
        stage1(d).wait_recv()
        for e in range(1, nl):
            stage2(d, e).start()
        to_sib(from_z(d), l).start()

    take(codes_in.at[q_rest], recv_b.at[1])
    take(atoms_in.at[:, l_rest], recv_b.at[0])

    got = codes_in[...].reshape(dev, LANES)
    pair_at = iota((1, pairs), 1)
    pair_src = fdiv(pair_at, cap)
    pair_j = pair_at - pair_src * cap
    j_hot = jnp.where(iota((LANES, pairs), 0) == pair_j, 1.0, 0.0).astype(BF16)
    src_hot = iota((dev, pairs), 0) == pair_src
    both = jnp.concatenate([got & 127, got >> 7], axis=0).astype(F32).astype(BF16)
    spread = nn(both, j_hot)
    low7 = jnp.sum(jnp.where(src_hot, spread[:dev], 0.0), axis=0, keepdims=True).astype(I32)
    high = jnp.sum(jnp.where(src_hot, spread[dev:], 0.0), axis=0, keepdims=True).astype(I32)
    pcode = low7 + (high << 7)
    valid_s[...] = jnp.where(pcode > 0, 1.0, 0.0)
    pcode = jnp.maximum(pcode - 1, 0)
    pslot = fdiv(pcode, local_q)
    pquery = pair_src * local_q + (pcode - pslot * local_q)
    onehot[...] = jnp.where(iota((own_rows, pairs), 0) == pslot, 1.0, 0.0).astype(BF16)
    qonehot[...] = jnp.where(iota((dev * local_q, pairs), 0) == pquery, 1.0, 0.0).astype(BF16)

    raw = atoms_in[...].reshape(dev, 2 * local_q, LANES).astype(F32)
    q_top = jnp.transpose(raw[:, :local_q].reshape(dev * local_q, LANES))
    q_low = jnp.transpose(raw[:, local_q:].reshape(dev * local_q, LANES))
    comps = prepare(q_top[:atoms], q_top[atoms:half], q_low[:atoms], q_low[atoms:half])
    for i in range(4):
        qprep[i * atoms : (i + 1) * atoms] = comps[i]

    def qself_step(g, carry):
        lanes = pl.ds(pl.multiple_of(g * LANES, LANES), LANES)
        qself[0:1, lanes] = self_overlap(qprep, lanes, atoms)
        return carry

    lax.fori_loop(0, dev * local_q // LANES, qself_step, 0)

    pad = jnp.zeros((7, own_rows), F32)
    hi_c, lo_c = split2(jnp.concatenate([confp[...], cself[...], pad], axis=0))
    pairs_c[...] = nn(hi_c, onehot[...]) + nn(lo_c, onehot[...])
    pad = jnp.zeros((7, dev * local_q), F32)
    hi_q, lo_q = split2(jnp.concatenate([qprep[...], qself[...], pad], axis=0))
    pairs_q[...] = nn(hi_q, qonehot[...]) + nn(lo_q, qonehot[...])

    def cross_step(g, carry):
        lanes = pl.ds(pl.multiple_of(g * LANES, LANES), LANES)
        cross = cross_overlap(pairs_q, pairs_c, lanes, atoms)
        selves = pairs_q[4 * atoms : 4 * atoms + 1, lanes] + pairs_c[4 * atoms : 4 * atoms + 1, lanes]
        shape_s[0:1, lanes] = cross / (selves - cross)
        return carry

    groups = pairs // LANES
    first = groups // 3
    lax.fori_loop(0, first, cross_step, 0)

    for d in range(1, nz):
        for e in range(1, nl):
            stage2(d, e).wait_recv()
            to_sib(from_z(d), from_l(e)).start()

    lax.fori_loop(first, groups, cross_step, 0)

    take(gath.at[:, pl.ds(0, nz * block), :], sib_recv)
    lib_copy.wait()

    rows = nq * block
    chunk = min(rows, 256)
    priors = None
    for r in range(0, rows, chunk):
        scores = None
        norms = None
        for k in range(nl):
            part = gath[k, r : r + chunk, :]
            prod = nt(part, lib[:, k * cols : (k + 1) * cols])
            wide = part.astype(F32)
            sq = jnp.sum(wide * wide, axis=1, keepdims=True)
            scores = prod if scores is None else scores + prod
            norms = sq if norms is None else norms + sq
        tv = (scores / (norms + EPSILON)).astype(BF16)
        tv_ref[r : r + chunk, :] = tv
        chosen = nn(tv, onehot[...]) * qonehot[r : r + chunk, :].astype(F32)
        chosen = jnp.sum(chosen, axis=0, keepdims=True)
        priors = chosen if priors is None else priors + chosen

    score = jnp.where(valid_s[...] > 0.0, shape_s[...] + priors, 0.0)
    hi_s, lo_s = split2(jnp.where(src_hot, score, 0.0))
    back = nt(hi_s, j_hot) + nt(lo_s, j_hot)
    for s in range(dev):
        ret_out[s // nl, s % nl] = back[s : s + 1]

    for t in qry_peers:
        remote(ret_out.at[t], mid_back.at[q], send_a.at[2], recv_a.at[2], t, l).start()
    mid_back[q] = ret_out[q]
    take(mid_back.at[q_rest], recv_a.at[2])
    for t in lib_peers:
        remote(mid_back.at[:, t], ret_in.at[l], send_b.at[2], recv_b.at[2], q, t).start()
    for k in range(nq):
        ret_in[l, k] = mid_back[k, l]

    take(gath.at[0, pl.ds(0, (nz - 1) * block), :], s1_send)
    take(gath.at[pl.ds(0, nl - 1), pl.ds(0, (nz - 1) * block), :], s2_send)
    take(gath.at[:, pl.ds(0, nz * block), :], sib_send)
    take(atoms_in.at[q_rest, 0], send_a.at[0])
    take(mid.at[l_rest], send_a.at[1])
    take(mid_back.at[q_rest], send_a.at[2])
    take(atoms_in.at[:, l_rest], send_b.at[0])
    take(codes_in.at[q_rest], send_b.at[1])
    take(ret_in.at[l_rest], recv_b.at[2])

    came = jnp.transpose(ret_in[...].reshape(dev, LANES))
    hi_b, lo_b = split2(came)
    mine = nn(hi_b, owns_b) + nn(lo_b, owns_b)
    final = jnp.sum(jnp.where(rank_hot, mine, 0.0), axis=0, keepdims=True)
    for i in range(local_q):
        line = final[:, i * listed : (i + 1) * listed]
        live = iota((1, listed), 1) < count_ref[i]
        out_ref[i : i + 1, :] = jnp.where(live, line, 0.0)

    take(ret_in.at[l_rest], send_b.at[2])


def body(nq, nl, query_prints, library_prints, query_atoms, conformer_atoms, candidates, candidate_count, home_row):
    dev = nq * nl
    block, width = query_prints.shape
    own_rows = library_prints.shape[0]
    local_q, listed = candidates.shape
    atoms = query_atoms.shape[1] // 4
    cand_n = local_q * listed
    cap = 2 * ((cand_n + dev - 1) // dev) + 4
    pairs = (dev * cap + LANES - 1) // LANES * LANES
    id_bytes = ((home_row.shape[0] - 1).bit_length() + 7) // 8
    rows = nq * block
    nz = nq // CORES
    limit = 56 * 1024 * 1024
    vm = pltpu.VMEM
    dma = pltpu.SemaphoreType.DMA
    vspec = pl.BlockSpec(memory_space=pltpu.VMEM)
    return pl.pallas_call(
        functools.partial(kernel, nq, nl, cap, id_bytes),
        out_shape=(
            jax.ShapeDtypeStruct((rows, own_rows), BF16),
            jax.ShapeDtypeStruct((local_q, listed), F32),
        ),
        in_specs=[pl.BlockSpec(memory_space=pltpu.HBM)] * 7,
        out_specs=(vspec, vspec),
        scratch_shapes=[
            vm((block, width), BF16),
            vm((local_q, 4 * atoms), F32),
            vm((local_q, listed), I32),
            pltpu.SMEM((local_q,), I32),
            vm((home_row.shape[0] // LANES, LANES), I32),
            vm((own_rows, width), BF16),
            vm((4 * atoms, own_rows), F32),
            vm((nl, rows, width // nl), BF16),
            vm((2 * local_q, LANES), BF16),
            vm((nq, nl, 2 * local_q, LANES), BF16),
            vm((nl, nq, 1, LANES), I32),
            vm((nl, nq, 1, LANES), I32),
            vm((nq, nl, 1, LANES), I32),
            vm((nq, nl, 1, LANES), F32),
            vm((nq, nl, 1, LANES), F32),
            vm((nl, nq, 1, LANES), F32),
            vm((4 * atoms, own_rows), F32),
            vm((4 * atoms, rows), F32),
            vm((4 * atoms + 8, pairs), F32),
            vm((4 * atoms + 8, pairs), F32),
            vm((own_rows, pairs), BF16),
            vm((rows, pairs), BF16),
            vm((1, own_rows), F32),
            vm((1, rows), F32),
            vm((1, pairs), F32),
            vm((1, pairs), F32),
            dma((7,)),
            dma, dma((nz,)),
            dma, dma,
            dma, dma((nz, nl)),
            dma((3,)), dma((3,)),
            dma((3,)), dma((3,)),
        ],
        compiler_params=pltpu.CompilerParams(
            collective_id=0, has_side_effects=True, vmem_limit_bytes=limit
        ),
    )(
        query_prints, library_prints, query_atoms, conformer_atoms.T, candidates, candidate_count,
        home_row.reshape(-1, LANES),
    )


def solution(mesh):
    return jax.shard_map(
        functools.partial(body, mesh.shape["qry"], mesh.shape["lib"]),
        mesh=mesh,
        in_specs=(
            P("qry", None),
            P(("lib", "qry"), None),
            P(("qry", "lib"), None),
            P(("lib", "qry"), None),
            P(("qry", "lib"), None),
            P(("qry", "lib")),
            P(),
        ),
        out_specs=(P(None, ("lib", "qry")), P(("qry", "lib"), None)),
        check_vma=False,
    )
```

```python
import functools
import math

import jax
import jax.numpy as jnp
from jax import lax
from jax.experimental import pallas as pl
from jax.experimental.pallas import tpu as pltpu
from jax.sharding import PartitionSpec as P

SHARPNESS = 0.8
EPSILON = 1e-06
LANES = 128
CORES = 2
SCALE = SHARPNESS * math.log2(math.e)
ROOT = math.sqrt(2.0 * SCALE)

F32 = jnp.float32
BF16 = jnp.bfloat16
I32 = jnp.int32


def nt(a, b):
    return lax.dot_general(a, b, (((1,), (1,)), ((), ())), preferred_element_type=F32)


def nn(a, b):
    return lax.dot_general(a, b, (((1,), (0,)), ((), ())), preferred_element_type=F32)


def split2(x):
    hi = x.astype(BF16)
    return hi, (x - hi.astype(F32)).astype(BF16)


def iota(shape, dim):
    return lax.broadcasted_iota(I32, shape, dim)


def fdiv(x, by):
    return jnp.floor((x.astype(F32) + 0.5) * (1.0 / by)).astype(I32)


def prepare(x, y, z, w):
    norm = SCALE * (x * x + y * y + z * z)
    return x * ROOT, y * ROOT, z * ROOT, w * jnp.exp2(-norm)


def self_overlap(ref, lanes, atoms):
    blocks = atoms // 8
    comp = [[ref[pl.ds(c * atoms + 8 * i, 8), lanes] for i in range(blocks)] for c in range(4)]
    total = None
    diag = [None] * blocks
    off = [None] * blocks
    for a in range(atoms):
        xa, ya, za, wa = (ref[pl.ds(c * atoms + a, 1), lanes] for c in range(4))
        wa2 = wa + wa
        for i in range(a // 8, blocks):
            e = jnp.exp2(xa * comp[0][i] + ya * comp[1][i] + za * comp[2][i])
            if i == a // 8:
                diag[i] = wa * e if diag[i] is None else diag[i] + wa * e
            else:
                off[i] = wa2 * e if off[i] is None else off[i] + wa2 * e
    for i in range(blocks):
        part = diag[i] if off[i] is None else diag[i] + off[i]
        part = part * comp[3][i]
        total = part if total is None else total + part
    return jnp.sum(total, axis=0, keepdims=True)


def cross_overlap(qref, cref, lanes, atoms):
    comp = [cref[pl.ds(c * atoms, atoms), lanes] for c in range(4)]
    acc = None
    for a in range(atoms):
        xa, ya, za, wa = (qref[pl.ds(c * atoms + a, 1), lanes] for c in range(4))
        e = wa * jnp.exp2(xa * comp[0] + ya * comp[1] + za * comp[2])
        acc = e if acc is None else acc + e
    return jnp.sum(acc * comp[3], axis=0, keepdims=True)


def kernel(
    nq, nl, cap, id_bytes,
    qp_hbm, lib_hbm, qa_hbm, conf_hbm, cand_hbm, count_hbm, home_hbm,
    tv_hbm, out_ref,
    tv_ref,
    qp_ref, qa_ref, cand_ref, count_ref, home_ref,
    lib, conf, gath, pack, atoms_in, bucket, mid, codes_in, ret_out, mid_back, ret_in,
    confp, qprep, pairs_c, pairs_q, onehot, qonehot, cself, qself, shape_s, valid_s,
    loc_sem, s1_send, s1_recv, sib_send, sib_recv, s2_send, s2_recv,
    send_a, recv_a, send_b, recv_b,
):
    q = lax.axis_index("qry")
    l = lax.axis_index("lib")
    dev = nq * nl
    me = q * nl + l
    nz = nq // CORES
    z, c = q // CORES, lax.rem(q, CORES)
    sib = z * CORES + (1 - c)
    own_rows = lib.shape[0]
    block = qp_ref.shape[0]
    cols = gath.shape[2]
    local_q, listed = cand_ref.shape
    cand_n = local_q * listed
    atoms = qa_ref.shape[1] // 4
    half = 2 * atoms
    pairs = onehot.shape[1]

    def wrap(x, n):
        return jnp.where(x >= n, x - n, x)

    lib_peers = [wrap(l + e, nl) for e in range(1, nl)]
    qry_peers = [wrap(q + d, nq) for d in range(1, nq)]

    def take(ref, sem):
        pltpu.make_async_copy(ref, ref, sem).wait()

    barrier = pltpu.get_barrier_semaphore()

    for tq, tl in [(q, t) for t in lib_peers] + [(t, l) for t in qry_peers]:
        pl.semaphore_signal(
            barrier, inc=1, device_id={"qry": tq, "lib": tl}, device_id_type=pl.DeviceIdType.MESH
        )

    loads = [
        pltpu.make_async_copy(src, dst, loc_sem.at[2 + n])
        for n, (src, dst) in enumerate(
            ((qa_hbm, qa_ref), (cand_hbm, cand_ref), (home_hbm, home_ref), (qp_hbm, qp_ref), (count_hbm, count_ref))
        )
    ]
    for load in loads:
        load.start()
    lib_copy = pltpu.make_async_copy(lib_hbm, lib, loc_sem.at[0])
    conf_copy = pltpu.make_async_copy(conf_hbm, conf, loc_sem.at[1])
    conf_copy.start()
    lib_copy.start()

    for load in loads:
        load.wait()

    qa = qa_ref[...]
    zero = jnp.zeros((local_q, LANES - half), F32)
    top = jnp.concatenate([qa[:, :half], zero], axis=1)
    low = jnp.concatenate([qa[:, half:], zero], axis=1)
    pack[...] = jnp.concatenate([top, low], axis=0).astype(BF16)

    ids = jnp.concatenate([cand_ref[pl.ds(i, 1), :] for i in range(local_q)], axis=1)
    table = home_ref[...]
    trows = table.shape[0]
    pieces = [
        jnp.transpose(((table >> (8 * k)) & 255).astype(F32)).astype(BF16) for k in range(id_bytes)
    ]
    row_hot = jnp.where(iota((trows, cand_n), 0) == (ids >> 7), 1.0, 0.0).astype(BF16)
    lane_hot = iota((LANES, cand_n), 0) == (ids & 127)
    stored = jnp.zeros((1, cand_n), I32)
    for k in range(id_bytes):
        found = nn(pieces[k], row_hot)
        byte = jnp.sum(jnp.where(lane_hot, found, 0.0), axis=0, keepdims=True)
        stored = stored + (byte.astype(I32) << (8 * k))
    owner = fdiv(stored, own_rows)
    slot = stored - owner * own_rows

    pl.semaphore_wait(barrier, nq + nl - 2)

    def remote(src, dst, ssem, rsem, dq, dl):
        return pltpu.make_async_remote_copy(
            src_ref=src, dst_ref=dst, send_sem=ssem, recv_sem=rsem,
            device_id={"qry": dq, "lib": dl}, device_id_type=pl.DeviceIdType.MESH,
        )

    def piece(bq, k):
        return gath.at[k, pl.ds(pl.multiple_of(bq * block, block), block), :]

    def stage1(d):
        return remote(
            qp_ref.at[:, pl.ds(pl.multiple_of(l * cols, cols), cols)], piece(q, l),
            s1_send, s1_recv.at[d], lax.rem(z + d, nz) * CORES + c, l,
        )

    def from_z(d):
        return lax.rem(z - d + nz, nz) * CORES + c

    def stage2(d, e):
        there = piece(from_z(d), l)
        return remote(there, there, s2_send, s2_recv.at[d, e], q, lax.rem(l + e, nl))

    def to_sib(bq, k):
        there = piece(bq, k)
        return remote(there, there, sib_send, sib_recv, sib, l)

    def from_l(e):
        return lax.rem(l - e + nl, nl)

    for d in range(1, nz):
        stage1(d).start()
    for k in range(nl):
        gath[k, pl.ds(pl.multiple_of(q * block, block), block), :] = qp_ref[:, k * cols : (k + 1) * cols]
    for k in range(nl):
        to_sib(q, k).start()

    for t in qry_peers:
        remote(pack, atoms_in.at[q, l], send_a.at[0], recv_a.at[0], t, l).start()
    atoms_in[q, l] = pack[...]

    owns = iota((dev, cand_n), 0) == owner
    owns_b = jnp.where(owns, 1.0, 0.0).astype(BF16)
    tri = jnp.where(iota((cand_n, cand_n), 0) < iota((cand_n, cand_n), 1), 1.0, 0.0).astype(BF16)
    before = nn(owns_b, tri)
    rank = jnp.sum(jnp.where(owns, before, 0.0), axis=0, keepdims=True).astype(I32)
    rank_hot = iota((LANES, cand_n), 0) == rank
    rank_b = jnp.where(rank_hot, 1.0, 0.0).astype(BF16)
    code = slot * local_q + fdiv(iota((1, cand_n), 1), listed) + 1
    lo = (code & 127).astype(F32)
    hi = (code >> 7).astype(F32)
    left = jnp.concatenate([jnp.where(owns, lo, 0.0), jnp.where(owns, hi, 0.0)], axis=0).astype(BF16)
    sums = nt(left, rank_b).astype(I32)
    codes = sums[:dev] + (sums[dev:] << 7)
    for o in range(dev):
        bucket[o // nq, o % nq] = codes[o : o + 1]

    for t in lib_peers:
        remote(bucket.at[t], mid.at[l], send_a.at[1], recv_a.at[1], q, t).start()
    mid[l] = bucket[l]

    conf_copy.wait()
    comps = prepare(*(conf[i * atoms : (i + 1) * atoms] for i in range(4)))
    for i in range(4):
        confp[i * atoms : (i + 1) * atoms] = comps[i]

    q_rest = pl.ds(0, nq - 1)
    l_rest = pl.ds(0, nl - 1)
    take(atoms_in.at[q_rest, 0], recv_a.at[0])
    for t in lib_peers:
        remote(atoms_in.at[:, l], atoms_in.at[:, l], send_b.at[0], recv_b.at[0], q, t).start()
    take(mid.at[l_rest], recv_a.at[1])
    for t in qry_peers:
        remote(mid.at[:, t], codes_in.at[q], send_b.at[1], recv_b.at[1], t, l).start()
    for k in range(nl):
        codes_in[q, k] = mid[k, q]

    def self_step(g, carry):
        lanes = pl.ds(pl.multiple_of(g * LANES, LANES), LANES)
        cself[0:1, lanes] = self_overlap(confp, lanes, atoms)
        return carry

    lax.fori_loop(0, own_rows // LANES, self_step, 0)

    for d in range(1, nz):
        stage1(d).wait_recv()
        for e in range(1, nl):
            stage2(d, e).start()
        to_sib(from_z(d), l).start()

    take(codes_in.at[q_rest], recv_b.at[1])
    take(atoms_in.at[:, l_rest], recv_b.at[0])

    got = codes_in[...].reshape(dev, LANES)
    pair_at = iota((1, pairs), 1)
    pair_src = fdiv(pair_at, cap)
    pair_j = pair_at - pair_src * cap
    j_hot = jnp.where(iota((LANES, pairs), 0) == pair_j, 1.0, 0.0).astype(BF16)
    src_hot = iota((dev, pairs), 0) == pair_src
    both = jnp.concatenate([got & 127, got >> 7], axis=0).astype(F32).astype(BF16)
    spread = nn(both, j_hot)
    low7 = jnp.sum(jnp.where(src_hot, spread[:dev], 0.0), axis=0, keepdims=True).astype(I32)
    high = jnp.sum(jnp.where(src_hot, spread[dev:], 0.0), axis=0, keepdims=True).astype(I32)
    pcode = low7 + (high << 7)
    valid_s[...] = jnp.where(pcode > 0, 1.0, 0.0)
    pcode = jnp.maximum(pcode - 1, 0)
    pslot = fdiv(pcode, local_q)
    pquery = pair_src * local_q + (pcode - pslot * local_q)
    onehot[...] = jnp.where(iota((own_rows, pairs), 0) == pslot, 1.0, 0.0).astype(BF16)
    qonehot[...] = jnp.where(iota((dev * local_q, pairs), 0) == pquery, 1.0, 0.0).astype(BF16)

    raw = atoms_in[...].reshape(dev, 2 * local_q, LANES).astype(F32)
    q_top = jnp.transpose(raw[:, :local_q].reshape(dev * local_q, LANES))
    q_low = jnp.transpose(raw[:, local_q:].reshape(dev * local_q, LANES))
    comps = prepare(q_top[:atoms], q_top[atoms:half], q_low[:atoms], q_low[atoms:half])
    for i in range(4):
        qprep[i * atoms : (i + 1) * atoms] = comps[i]

    def qself_step(g, carry):
        lanes = pl.ds(pl.multiple_of(g * LANES, LANES), LANES)
        qself[0:1, lanes] = self_overlap(qprep, lanes, atoms)
        return carry

    lax.fori_loop(0, dev * local_q // LANES, qself_step, 0)

    pad = jnp.zeros((7, own_rows), F32)
    hi_c, lo_c = split2(jnp.concatenate([confp[...], cself[...], pad], axis=0))
    pairs_c[...] = nn(hi_c, onehot[...]) + nn(lo_c, onehot[...])
    pad = jnp.zeros((7, dev * local_q), F32)
    hi_q, lo_q = split2(jnp.concatenate([qprep[...], qself[...], pad], axis=0))
    pairs_q[...] = nn(hi_q, qonehot[...]) + nn(lo_q, qonehot[...])

    def cross_step(g, carry):
        lanes = pl.ds(pl.multiple_of(g * LANES, LANES), LANES)
        cross = cross_overlap(pairs_q, pairs_c, lanes, atoms)
        selves = pairs_q[4 * atoms : 4 * atoms + 1, lanes] + pairs_c[4 * atoms : 4 * atoms + 1, lanes]
        shape_s[0:1, lanes] = cross / (selves - cross)
        return carry

    groups = pairs // LANES
    first = groups // 3
    lax.fori_loop(0, first, cross_step, 0)

    for d in range(1, nz):
        for e in range(1, nl):
            stage2(d, e).wait_recv()
            to_sib(from_z(d), from_l(e)).start()

    lax.fori_loop(first, groups, cross_step, 0)

    take(gath.at[:, pl.ds(0, nz * block), :], sib_recv)
    lib_copy.wait()

    rows = nq * block
    chunk = min(rows, 256)
    priors = None
    for r in range(0, rows, chunk):
        scores = None
        norms = None
        for k in range(nl):
            part = gath[k, r : r + chunk, :]
            prod = nt(part, lib[:, k * cols : (k + 1) * cols])
            wide = part.astype(F32)
            sq = jnp.sum(wide * wide, axis=1, keepdims=True)
            scores = prod if scores is None else scores + prod
            norms = sq if norms is None else norms + sq
        tv = (scores * (1.0 / (norms + EPSILON))).astype(BF16)
        tv_ref[r : r + chunk, :] = tv
        chosen = nn(tv, onehot[...]) * qonehot[r : r + chunk, :].astype(F32)
        chosen = jnp.sum(chosen, axis=0, keepdims=True)
        priors = chosen if priors is None else priors + chosen

    tv_copy = pltpu.make_async_copy(tv_ref, tv_hbm, loc_sem.at[7])
    tv_copy.start()
    score = jnp.where(valid_s[...] > 0.0, shape_s[...] + priors, 0.0)
    hi_s, lo_s = split2(jnp.where(src_hot, score, 0.0))
    back = nt(hi_s, j_hot) + nt(lo_s, j_hot)
    for s in range(dev):
        ret_out[s // nl, s % nl] = back[s : s + 1]

    for t in qry_peers:
        remote(ret_out.at[t], mid_back.at[q], send_a.at[2], recv_a.at[2], t, l).start()
    mid_back[q] = ret_out[q]
    take(mid_back.at[q_rest], recv_a.at[2])
    for t in lib_peers:
        remote(mid_back.at[:, t], ret_in.at[l], send_b.at[2], recv_b.at[2], q, t).start()
    for k in range(nq):
        ret_in[l, k] = mid_back[k, l]

    take(gath.at[0, pl.ds(0, (nz - 1) * block), :], s1_send)
    take(gath.at[pl.ds(0, nl - 1), pl.ds(0, (nz - 1) * block), :], s2_send)
    take(gath.at[:, pl.ds(0, nz * block), :], sib_send)
    take(atoms_in.at[q_rest, 0], send_a.at[0])
    take(mid.at[l_rest], send_a.at[1])
    take(mid_back.at[q_rest], send_a.at[2])
    take(atoms_in.at[:, l_rest], send_b.at[0])
    take(codes_in.at[q_rest], send_b.at[1])
    take(ret_in.at[l_rest], recv_b.at[2])

    came = jnp.transpose(ret_in[...].reshape(dev, LANES))
    hi_b, lo_b = split2(came)
    mine = nn(hi_b, owns_b) + nn(lo_b, owns_b)
    final = jnp.sum(jnp.where(rank_hot, mine, 0.0), axis=0, keepdims=True)
    for i in range(local_q):
        line = final[:, i * listed : (i + 1) * listed]
        live = iota((1, listed), 1) < count_ref[i]
        out_ref[i : i + 1, :] = jnp.where(live, line, 0.0)

    take(ret_in.at[l_rest], send_b.at[2])
    tv_copy.wait()


def body(nq, nl, query_prints, library_prints, query_atoms, conformer_atoms, candidates, candidate_count, home_row):
    dev = nq * nl
    block, width = query_prints.shape
    own_rows = library_prints.shape[0]
    local_q, listed = candidates.shape
    atoms = query_atoms.shape[1] // 4
    cand_n = local_q * listed
    cap = 2 * ((cand_n + dev - 1) // dev) + 4
    pairs = (dev * cap + LANES - 1) // LANES * LANES
    id_bytes = ((home_row.shape[0] - 1).bit_length() + 7) // 8
    rows = nq * block
    nz = nq // CORES
    limit = 56 * 1024 * 1024
    vm = pltpu.VMEM
    dma = pltpu.SemaphoreType.DMA
    vspec = pl.BlockSpec(memory_space=pltpu.VMEM)
    return pl.pallas_call(
        functools.partial(kernel, nq, nl, cap, id_bytes),
        out_shape=(
            jax.ShapeDtypeStruct((rows, own_rows), BF16),
            jax.ShapeDtypeStruct((local_q, listed), F32),
        ),
        in_specs=[pl.BlockSpec(memory_space=pltpu.HBM)] * 7,
        out_specs=(pl.BlockSpec(memory_space=pl.ANY), vspec),
        scratch_shapes=[
            vm((rows, own_rows), BF16),
            vm((block, width), BF16),
            vm((local_q, 4 * atoms), F32),
            vm((local_q, listed), I32),
            pltpu.SMEM((local_q,), I32),
            vm((home_row.shape[0] // LANES, LANES), I32),
            vm((own_rows, width), BF16),
            vm((4 * atoms, own_rows), F32),
            vm((nl, rows, width // nl), BF16),
            vm((2 * local_q, LANES), BF16),
            vm((nq, nl, 2 * local_q, LANES), BF16),
            vm((nl, nq, 1, LANES), I32),
            vm((nl, nq, 1, LANES), I32),
            vm((nq, nl, 1, LANES), I32),
            vm((nq, nl, 1, LANES), F32),
            vm((nq, nl, 1, LANES), F32),
            vm((nl, nq, 1, LANES), F32),
            vm((4 * atoms, own_rows), F32),
            vm((4 * atoms, rows), F32),
            vm((4 * atoms + 8, pairs), F32),
            vm((4 * atoms + 8, pairs), F32),
            vm((own_rows, pairs), BF16),
            vm((rows, pairs), BF16),
            vm((1, own_rows), F32),
            vm((1, rows), F32),
            vm((1, pairs), F32),
            vm((1, pairs), F32),
            dma((8,)),
            dma, dma((nz,)),
            dma, dma,
            dma, dma((nz, nl)),
            dma((3,)), dma((3,)),
            dma((3,)), dma((3,)),
        ],
        compiler_params=pltpu.CompilerParams(
            collective_id=0, has_side_effects=True, vmem_limit_bytes=limit
        ),
    )(
        query_prints, library_prints, query_atoms, conformer_atoms.T, candidates, candidate_count,
        home_row.reshape(-1, LANES),
    )


def solution(mesh):
    return jax.shard_map(
        functools.partial(body, mesh.shape["qry"], mesh.shape["lib"]),
        mesh=mesh,
        in_specs=(
            P("qry", None),
            P(("lib", "qry"), None),
            P(("qry", "lib"), None),
            P(("lib", "qry"), None),
            P(("qry", "lib"), None),
            P(("qry", "lib")),
            P(),
        ),
        out_specs=(P(None, ("lib", "qry")), P(("qry", "lib"), None)),
        check_vma=False,
    )
```
